1024 devices in a mesh: node: 128 (over y, x, core), local: 8 (over z).
Axes of the slice: x: 8, y: 8, z: 8, core: 2. Of those that a mesh axis runs over, the one named last changes fastest.
Arguments:
- expert_ids: int32 [4096, 8], P('node'), may hold values from 0 to 255, as said below
- slot_gates: float32 [128, 2, 256], P('node'), may hold values from 0 to 0.6, as said below
- expert_rows: bfloat16 [128, 256, 2, 7168], P('node', None, None, 'local'), may hold values from -6 to 6
- residual: bfloat16 [4096, 7168], P('node', 'local')
- norm_gain: float32 [7168], P('local'), may hold values from 0.25 to 1.75
- w_q_down: bfloat16 [7168, 1536], P('local'), may hold values from -0.0625 to 0.0625
- w_kv_down: bfloat16 [7168, 576], P('local'), may hold values from -0.0625 to 0.0625
Outputs:
- hidden: bfloat16 [4096, 7168], P('node', 'local')
- q_latent: bfloat16 [4096, 1536], P(('node', 'local'))
- kv_latent: bfloat16 [4096, 576], P(('node', 'local'))
The draws below stay inside these ranges and needn't reach their ends.
Inputs may be any that keep to these rules, and one draw needn't show every extreme that they name: `expert_ids`: each token names both experts of each of 4 different nodes; expert e lives on node e // 2. Of the tokens of one node, at most 2 use any one node, and exactly 2 use some node. `slot_gates`: slot s * 2 + j of node m serves the j-th token, in order, of node s that uses node m; its weights are positive, and zero on slots that serve no token.
All inputs are finite; a program needn't handle non-finite values.
Results may differ from the reference program's by a relative error of at most 0.0058.
Values may be sent and summed in bfloat16 or wider, within the bound.
A program may use at most 32 MiB of HBM per device.

```python
import math
import jax
import jax.numpy as jnp
from jax import lax

D = 7168
QL = 1536
KVL = 576
EXP_NODE = 2
NODES_TOK = 4
TOP = 8
TOK_NODE = 32
TOKENS = 4096
CAP = 2
SLOTS = 256
N_NODE = 128


def routing(key):
    groups = N_NODE // NODES_TOK
    pool_size = 2 * TOK_NODE

    def classes_of(subkey):
        key_one, key_two = jax.random.split(subkey)
        remaining = CAP + jax.random.permutation(key_one, pool_size - CAP)[:TOK_NODE - CAP]
        positions = jnp.concatenate([jnp.arange(CAP, dtype=jnp.int32), remaining.astype(jnp.int32)])
        positions = positions[jax.random.permutation(key_two, TOK_NODE)]
        return positions // CAP
    subkeys = jax.random.split(jax.random.fold_in(key, 101), N_NODE * NODES_TOK)
    classes = jax.vmap(classes_of)(subkeys).reshape(N_NODE, NODES_TOK, TOK_NODE)
    node_order = jax.vmap(lambda subkey: jax.random.permutation(subkey, N_NODE))(jax.random.split(jax.random.fold_in(key, 202), N_NODE)).astype(jnp.int32)
    chosen = jnp.arange(NODES_TOK, dtype=jnp.int32)[None, :, None] * groups + classes
    chosen_nodes = jnp.take_along_axis(node_order, chosen.reshape(N_NODE, NODES_TOK * TOK_NODE), axis=1).reshape(N_NODE, NODES_TOK, TOK_NODE)
    alike_class = classes[:, :, :, None] == classes[:, :, None, :]
    earlier = jnp.arange(TOK_NODE)[None, :] < jnp.arange(TOK_NODE)[:, None]
    slot_rank = jnp.sum((alike_class & earlier[None, None, :, :]).astype(jnp.int32), axis=-1)
    return (chosen_nodes, slot_rank)


def draw_expert_ids(key, part):
    chosen_nodes, slot_rank = routing(key)
    expert_table = chosen_nodes.transpose(0, 2, 1)[:, :, :, None] * EXP_NODE + jnp.arange(EXP_NODE, dtype=jnp.int32)[None, None, None, :]
    return expert_table.reshape(TOKENS, TOP).astype(jnp.int32)


def draw_slot_gates(key, part):
    chosen_nodes, slot_rank = routing(key)
    key = jax.random.fold_in(key, 11)
    entries = N_NODE * NODES_TOK * TOK_NODE
    values = jnp.exp(jax.random.uniform(key, (entries, EXP_NODE), jnp.float32, math.log(0.05), math.log(0.6)))
    source = jnp.broadcast_to(jnp.arange(N_NODE, dtype=jnp.int32)[:, None, None], chosen_nodes.shape)
    slot_index = (source * CAP + slot_rank).reshape(-1)
    target = chosen_nodes.reshape(-1)
    gates = jnp.zeros((N_NODE, SLOTS, EXP_NODE), jnp.float32).at[target, slot_index].set(values)
    return gates.transpose(0, 2, 1)


def draw_residual(key, part):
    key = jax.random.fold_in(key, 3)
    key_one, key_two = jax.random.split(key)
    column = jnp.arange(D, dtype=jnp.float32) / D
    noise = jnp.clip(jax.random.normal(key_one, (TOKENS, D), jnp.float32), -4.0, 4.0)
    spread = 3.0
    row_scale = 0.5 * jnp.exp(jax.random.uniform(key_two, (TOKENS, 1), jnp.float32, 0.0, math.log(10.0)))
    return (noise * row_scale * jnp.power(spread, column)[None, :]).astype(jnp.bfloat16)


def level_of(stream_key, shape, cuts, low, largest):
    loudness, own = 1.0, jax.random.fold_in(stream_key, 6)
    for position, shards_of in cuts:
        heights = jnp.exp(jax.random.uniform(jax.random.fold_in(own, position), (shards_of,), jnp.float32, low / len(cuts), largest / len(cuts)))
        loudness = loudness * jnp.repeat(heights, shape[position] // shards_of).reshape([-1 if axis == position else 1 for axis in range(len(shape))])
    return loudness


def centred(key, shape, deviation, most, cuts=(), kind=jnp.bfloat16):
    values = deviation * jax.random.normal(key, shape, jnp.float32)
    if cuts:
        values = values * level_of(key, shape, cuts, -0.22, 0.18)
    return jnp.clip(values, -most, most).astype(kind)


def setup_inputs(seed: int = 0) -> dict:
    arg_keys = jax.random.split(jax.random.key(seed), 8)
    expert_ids = draw_expert_ids(jax.random.fold_in(arg_keys[7], 71), 0)
    slot_gates = draw_slot_gates(jax.random.fold_in(arg_keys[7], 71), 0)
    expert_rows = centred(arg_keys[2], (N_NODE, SLOTS, EXP_NODE, D), 1.0, 6.0, ((0, 128), (3, 8)))
    residual = draw_residual(jax.random.fold_in(arg_keys[7], 71), 0)
    norm_gain = jnp.clip(1.0 + 0.15 * jax.random.normal(arg_keys[4], (D,), jnp.float32), 0.25, 1.75)
    w_q_down = centred(arg_keys[5], (D, QL), D ** -0.5, 0.0625, ((0, 8),))
    w_kv_down = centred(arg_keys[6], (D, KVL), D ** -0.5, 0.0625, ((0, 8),))
    return dict(expert_ids=expert_ids, slot_gates=slot_gates, expert_rows=expert_rows, residual=residual, norm_gain=norm_gain, w_q_down=w_q_down, w_kv_down=w_kv_down)


epsilon = 1e-06

def weighted_rows(pieces):
    gate_table, node_rows = pieces
    weighted = jnp.zeros((node_rows.shape[0], node_rows.shape[2]), jnp.float32)
    for expert in range(EXP_NODE):
        weighted = weighted + gate_table[expert][:, None] * node_rows[:, expert, :].astype(jnp.float32)
    return weighted.astype(jnp.bfloat16)

def reference(expert_ids, slot_gates, expert_rows, residual, norm_gain, w_q_down, w_kv_down):
    node_part = lax.map(weighted_rows, (slot_gates, expert_rows))
    id_blocks = expert_ids.reshape(N_NODE, TOK_NODE, TOP)
    res_blocks = residual.reshape(N_NODE, TOK_NODE, D)
    node_range = jnp.arange(N_NODE, dtype=jnp.int32)

    def owner_rows(pieces):
        source, id_rows, res_rows = pieces
        node_ids = id_rows // EXP_NODE
        routed = lax.optimization_barrier(jnp.max((node_ids[:, :, None] == node_range[None, None, :]).astype(jnp.int32), axis=1))
        slot_rank = jnp.cumsum(routed, axis=0) - routed
        slot_index = jnp.minimum(source * CAP + slot_rank, SLOTS - 1).astype(jnp.int32)
        picked = node_part[node_range[None, :], slot_index]
        combined = lax.optimization_barrier(jnp.sum(jnp.where(routed[:, :, None] == 1, picked.astype(jnp.float32), jnp.float32(0.0)), axis=1))
        return (res_rows.astype(jnp.float32) + combined).astype(jnp.bfloat16)
    hidden = lax.map(owner_rows, (node_range, id_blocks, res_blocks)).reshape(TOKENS, D)
    hidden_f = hidden.astype(jnp.float32)
    mean_square = lax.optimization_barrier(jnp.sum(hidden_f * hidden_f, axis=1)) / D
    normed = (hidden_f * lax.rsqrt(mean_square + epsilon)[:, None] * norm_gain).astype(jnp.bfloat16)
    q_latent = jnp.dot(normed, w_q_down, preferred_element_type=jnp.float32).astype(jnp.bfloat16)
    kv_latent = jnp.dot(normed, w_kv_down, preferred_element_type=jnp.float32).astype(jnp.bfloat16)
    return (hidden, q_latent, kv_latent)
```

```python
import jax
import jax.numpy as jnp
from jax import lax
from jax.experimental import pallas as pl
from jax.experimental.pallas import tpu as pltpu
from jax.sharding import PartitionSpec as P

D = 7168
QL = 1536
KVL = 576
TOK = 32
OWN = 4
NODES = 128
SLOTS = 256
COLS = 896
BLOCKS = COLS // 128
LAT_BLOCKS = 17
LOCALS = 8
HI_LANE = 64
LO_LANE = 96
EPSILON = 1e-06
f32, bf16 = jnp.float32, jnp.bfloat16
MESH = pl.DeviceIdType.MESH


def partner(me, k):
    dx, dy, dc = k & 7, (k + (k >> 3)) & 7, k >> 6
    y, x, c = me >> 4, (me >> 1) & 7, me & 1
    return (((y + dy) & 7) << 4) | (((x + dx) & 7) << 1) | ((c + dc) & 1)


def wait_bytes(ref, sem):
    pltpu.make_async_copy(ref, ref, sem).wait()


def kernel(
    ids_hbm, gates_hbm, rows_hbm, res_hbm, gain_hbm, wq_hbm, wkv_hbm,
    hid_out, q_out, kv_out,
    ids, gates, rows, res, gain, wq, wkv, send, recv, scaled, zsend, zrecv,
    in_sem, send_sem, recv_sem, zsend_sem, zrecv_sem,
):
    me = lax.axis_index("node")
    z = lax.axis_index("local")
    loads = [
        pltpu.make_async_copy(source, target, in_sem.at[i])
        for i, (source, target) in enumerate(
            [
                (gates_hbm.at[0], gates), (rows_hbm.at[0], rows), (ids_hbm, ids), (res_hbm, res),
                (gain_hbm, gain), (wq_hbm, wq), (wkv_hbm, wkv),
            ]
        )
    ]
    for load in loads:
        load.start()

    barrier = pltpu.get_barrier_semaphore()

    def greet(k, carry):
        pl.semaphore_signal(
            barrier, inc=1, device_id={"node": partner(me, k)}, device_id_type=MESH
        )
        return carry

    lax.fori_loop(1, NODES, greet, 0)
    for k in range(1, LOCALS):
        pl.semaphore_signal(barrier, inc=1, device_id={"local": (z + k) & 7}, device_id_type=MESH)

    loads[0].wait()
    gate_columns = jnp.concatenate([gates[...], jnp.zeros((6, SLOTS), f32)], axis=0).T
    loads[1].wait()
    pairs = rows[...].astype(f32)
    weighted = pairs[:, 0, :] * gate_columns[:, 0:1] + pairs[:, 1, :] * gate_columns[:, 1:2]
    send_rows = send.reshape(BLOCKS, SLOTS, 128)
    for block in range(BLOCKS):
        send_rows[block] = weighted[:, 128 * block : 128 * block + 128].astype(bf16)

    pl.semaphore_wait(barrier, NODES - 1 + LOCALS - 1)

    def push(k, carry):
        other = partner(me, k)
        pltpu.make_async_remote_copy(
            src_ref=send.at[:, other], dst_ref=recv.at[:, me], send_sem=send_sem, recv_sem=recv_sem,
            device_id={"node": other}, device_id_type=MESH,
        ).start()
        return carry

    lax.fori_loop(1, NODES, push, 0)
    pltpu.make_async_copy(send.at[:, me], recv.at[:, me], recv_sem).start()

    for load in loads[2:5]:
        load.wait()
    slot = lax.broadcasted_iota(jnp.int32, (SLOTS, TOK), 0)
    nodes = ids[...] >> 1
    routed = nodes[0:1, :] == (slot >> 1)
    for entry in range(1, 8):
        routed = routed | (nodes[entry : entry + 1, :] == (slot >> 1))
    earlier = (
        lax.broadcasted_iota(jnp.int32, (TOK, TOK), 0)
        < lax.broadcasted_iota(jnp.int32, (TOK, TOK), 1)
    ).astype(bf16)
    rank = jnp.dot(routed.astype(bf16), earlier, preferred_element_type=f32)
    serves = (routed & (rank == (slot & 1).astype(f32))).astype(bf16)

    wait_bytes(recv, recv_sem)
    recv_rows = recv.reshape(BLOCKS, SLOTS, 128)
    squares = jnp.zeros((TOK, 128), f32)
    for block in range(BLOCKS):
        cols = slice(128 * block, 128 * block + 128)
        combined = lax.dot_general(
            serves, recv_rows[block], (((0,), (0,)), ((), ())), preferred_element_type=f32
        )
        hidden = (res[:, cols].astype(f32) + combined).astype(bf16)
        hid_out[:, cols] = hidden
        hidden = hidden.astype(f32)
        squares = squares + hidden * hidden
        scaled[:, cols] = (hidden * gain[:, cols]).astype(bf16)

    loads[5].wait()
    loads[6].wait()
    zsend_rows = zsend.reshape(LAT_BLOCKS, TOK, 128)
    stream = scaled[...]
    query = jnp.dot(stream, wq[...], preferred_element_type=f32)
    for block in range(12):
        zsend_rows[block] = query[:, 128 * block : 128 * block + 128].astype(bf16)
    keys = lax.dot_general(stream, wkv[...], (((1,), (1,)), ((), ())), preferred_element_type=f32)
    for block in range(4):
        zsend_rows[12 + block] = keys[:, 128 * block : 128 * block + 128].astype(bf16)
    quarter = jnp.sum(squares, axis=1, keepdims=True) * 0.25
    high = quarter.astype(bf16)
    low = jnp.where(quarter < jnp.inf, quarter - high.astype(f32), 0.0).astype(bf16)
    zsend_rows[16] = jnp.concatenate(
        [
            keys[:, 512:576].astype(bf16),
            jnp.broadcast_to(high, (TOK, LO_LANE - HI_LANE)),
            jnp.broadcast_to(low, (TOK, 128 - LO_LANE)),
        ],
        axis=1,
    )
    for k in range(1, LOCALS):
        other = (z + k) & 7
        pltpu.make_async_remote_copy(
            src_ref=zsend.at[:, other], dst_ref=zrecv.at[z], send_sem=zsend_sem, recv_sem=zrecv_sem,
            device_id={"local": other}, device_id_type=MESH,
        ).start()
    pltpu.make_async_copy(zsend.at[:, z], zrecv.at[z], zrecv_sem).start()
    wait_bytes(send.at[:, pl.ds(0, NODES - 1)], send_sem)
    wait_bytes(zrecv, zrecv_sem)

    zrecv_rows = zrecv.reshape(LOCALS, LAT_BLOCKS * OWN, 128)
    total = zrecv_rows[0].astype(f32)
    for source in range(1, LOCALS):
        total = total + zrecv_rows[source].astype(f32)
    last = total[16 * OWN : 17 * OWN]
    square_sum = (last[:, HI_LANE : HI_LANE + 1] + last[:, LO_LANE : LO_LANE + 1]) * 4.0
    finite = square_sum < jnp.inf
    inverse = lax.rsqrt(square_sum / D + EPSILON)
    for block in range(LAT_BLOCKS):
        part = total[OWN * block : OWN * block + OWN]
        part = jnp.where(finite, part * inverse, 0.0).astype(bf16)
        if block < 12:
            q_out[:, 128 * block : 128 * block + 128] = part
        elif block < 16:
            kv_out[:, 128 * block - QL : 128 * block - QL + 128] = part
        else:
            kv_out[:, 512:576] = part[:, 0:64]
    wait_bytes(zrecv.at[pl.ds(0, LOCALS - 1)], zsend_sem)


def on_device(expert_ids, slot_gates, expert_rows, residual, norm_gain, w_q_down, w_kv_down):
    anywhere = pl.BlockSpec(memory_space=pl.ANY)
    vmem = pl.BlockSpec(memory_space=pltpu.VMEM)
    return pl.pallas_call(
        kernel,
        out_shape=(
            jax.ShapeDtypeStruct((TOK, COLS), bf16),
            jax.ShapeDtypeStruct((OWN, QL), bf16),
            jax.ShapeDtypeStruct((OWN, KVL), bf16),
        ),
        in_specs=[anywhere] * 7,
        out_specs=(vmem,) * 3,
        scratch_shapes=[
            pltpu.VMEM((8, TOK), jnp.int32),
            pltpu.VMEM((2, SLOTS), f32),
            pltpu.VMEM((SLOTS, 2, COLS), bf16),
            pltpu.VMEM((TOK, COLS), bf16),
            pltpu.VMEM((1, COLS), f32),
            pltpu.VMEM((COLS, QL), bf16),
            pltpu.VMEM((KVL, COLS), bf16),
            pltpu.VMEM((BLOCKS, NODES, 2, 128), bf16),
            pltpu.VMEM((BLOCKS, NODES, 2, 128), bf16),
            pltpu.VMEM((TOK, COLS), bf16),
            pltpu.VMEM((LAT_BLOCKS, LOCALS, OWN, 128), bf16),
            pltpu.VMEM((LOCALS, LAT_BLOCKS, OWN, 128), bf16),
            pltpu.SemaphoreType.DMA((7,)),
            pltpu.SemaphoreType.DMA,
            pltpu.SemaphoreType.DMA,
            pltpu.SemaphoreType.DMA,
            pltpu.SemaphoreType.DMA,
        ],
        compiler_params=pltpu.CompilerParams(
            collective_id=0, has_side_effects=True, vmem_limit_bytes=56 * 1024 * 1024
        ),
        name="combine_norm_project",
    )(
        expert_ids.T, slot_gates, expert_rows, residual, norm_gain.reshape(1, COLS), w_q_down,
        w_kv_down.T,
    )


def solution(mesh):
    return jax.shard_map(
        on_device,
        mesh=mesh,
        in_specs=(
            P("node", None),
            P("node", None, None),
            P("node", None, None, "local"),
            P("node", "local"),
            P("local"),
            P("local", None),
            P("local", None),
        ),
        out_specs=(P("node", "local"), P(("node", "local"), None), P(("node", "local"), None)),
        check_vma=False,
    )
```

```python
import jax
import jax.numpy as jnp
from jax import lax
from jax.experimental import pallas as pl
from jax.experimental.pallas import tpu as pltpu
from jax.sharding import PartitionSpec as P

D = 7168
QL = 1536
KVL = 576
TOK = 32
OWN = 4
NODES = 128
SLOTS = 256
COLS = 896
BLOCKS = COLS // 128
LAT_BLOCKS = 17
LOCALS = 8
HI_LANE = 64
LO_LANE = 96
EPSILON = 1e-06
f32, bf16 = jnp.float32, jnp.bfloat16
MESH = pl.DeviceIdType.MESH


def hops(shift):
    return min(shift, 8 - shift)


SHIFTS = sorted(
    ((y, x) for y in range(8) for x in range(8) if (y, x) != (0, 0)),
    key=lambda shift: (-hops(shift[0]) - hops(shift[1]), (shift[0] * 3 + shift[1] * 5) % 8),
)
PER_WORD = 5
WORDS = [
    (
        sum((8 * y + x) << (6 * place) for place, (y, x) in enumerate(SHIFTS[at : at + PER_WORD])),
        len(SHIFTS[at : at + PER_WORD]),
    )
    for at in range(0, len(SHIFTS), PER_WORD)
]
RING = (4, 3, 5, 2, 6, 1, 7)


def for_others(me, visit):
    y, x = me >> 4, (me >> 1) & 7
    for word, count in WORDS:

        def step(place, carry, word=word):
            shift = (jnp.int32(word) >> (6 * place)) & 63
            chip = (((y + (shift >> 3)) & 7) << 4) | (((x + shift) & 7) << 1)
            visit(chip | ((me + 1) & 1))
            visit(chip | (me & 1))
            return carry

        lax.fori_loop(0, count, step, 0)
    visit(me ^ 1)


def wait_bytes(ref, sem):
    pltpu.make_async_copy(ref, ref, sem).wait()


def kernel(
    ids_hbm, gates_hbm, rows_hbm, res_hbm, gain_hbm, wq_hbm, wkv_hbm,
    hid_out, q_out, kv_out,
    ids, gates, rows, res, gain, wq, wkv, send, recv, scaled, zsend, zrecv,
    in_sem, send_sem, recv_sem, zsend_sem, zrecv_sem,
):
    me = lax.axis_index("node")
    z = lax.axis_index("local")
    loads = [
        pltpu.make_async_copy(source, target, in_sem.at[i])
        for i, (source, target) in enumerate(
            [
                (gates_hbm.at[0], gates), (rows_hbm.at[0], rows), (ids_hbm, ids), (res_hbm, res),
                (gain_hbm, gain), (wq_hbm, wq), (wkv_hbm, wkv),
            ]
        )
    ]
    for load in loads:
        load.start()

    barrier = pltpu.get_barrier_semaphore()

    def greet(other):
        pl.semaphore_signal(barrier, inc=1, device_id={"node": other}, device_id_type=MESH)

    for_others(me, greet)
    for k in RING:
        pl.semaphore_signal(barrier, inc=1, device_id={"local": (z + k) & 7}, device_id_type=MESH)

    loads[0].wait()
    gate_columns = jnp.concatenate([gates[...], jnp.zeros((6, SLOTS), f32)], axis=0).T
    loads[1].wait()
    pairs = rows[...].astype(f32)
    weighted = pairs[:, 0, :] * gate_columns[:, 0:1] + pairs[:, 1, :] * gate_columns[:, 1:2]
    send_rows = send.reshape(BLOCKS, SLOTS, 128)
    for block in range(BLOCKS):
        send_rows[block] = weighted[:, 128 * block : 128 * block + 128].astype(bf16)

    pl.semaphore_wait(barrier, NODES - 1 + LOCALS - 1)

    def push(other):
        pltpu.make_async_remote_copy(
            src_ref=send.at[:, other], dst_ref=recv.at[:, me], send_sem=send_sem, recv_sem=recv_sem,
            device_id={"node": other}, device_id_type=MESH,
        ).start()

    for_others(me, push)
    pltpu.make_async_copy(send.at[:, me], recv.at[:, me], recv_sem).start()

    for load in loads[2:5]:
        load.wait()
    slot = lax.broadcasted_iota(jnp.int32, (SLOTS, TOK), 0)
    nodes = ids[...] >> 1
    routed = nodes[0:1, :] == (slot >> 1)
    for entry in range(1, 8):
        routed = routed | (nodes[entry : entry + 1, :] == (slot >> 1))
    earlier = (
        lax.broadcasted_iota(jnp.int32, (TOK, TOK), 0)
        < lax.broadcasted_iota(jnp.int32, (TOK, TOK), 1)
    ).astype(bf16)
    rank = jnp.dot(routed.astype(bf16), earlier, preferred_element_type=f32)
    serves = (routed & (rank == (slot & 1).astype(f32))).astype(bf16)

    wait_bytes(recv, recv_sem)
    recv_rows = recv.reshape(BLOCKS, SLOTS, 128)
    squares = jnp.zeros((TOK, 128), f32)
    for block in range(BLOCKS):
        cols = slice(128 * block, 128 * block + 128)
        combined = lax.dot_general(
            serves, recv_rows[block], (((0,), (0,)), ((), ())), preferred_element_type=f32
        )
        hidden = (res[:, cols].astype(f32) + combined).astype(bf16)
        hid_out[:, cols] = hidden
        hidden = hidden.astype(f32)
        squares = squares + hidden * hidden
        scaled[:, cols] = (hidden * gain[cols][None, :]).astype(bf16)

    loads[5].wait()
    zsend_rows = zsend.reshape(LAT_BLOCKS, TOK, 128)

    def pass_on(blocks):
        for k in RING:
            other = (z + k) & 7
            pltpu.make_async_remote_copy(
                src_ref=zsend.at[blocks, other], dst_ref=zrecv.at[z, blocks], send_sem=zsend_sem,
                recv_sem=zrecv_sem, device_id={"local": other}, device_id_type=MESH,
            ).start()
        pltpu.make_async_copy(zsend.at[blocks, z], zrecv.at[z, blocks], zrecv_sem).start()

    stream = scaled[...]
    query = jnp.dot(stream, wq[:, 0:1024], preferred_element_type=f32)
    for block in range(8):
        zsend_rows[block] = query[:, 128 * block : 128 * block + 128].astype(bf16)
    pass_on(pl.ds(0, 8))
    query = jnp.dot(stream, wq[:, 1024:QL], preferred_element_type=f32)
    for block in range(4):
        zsend_rows[8 + block] = query[:, 128 * block : 128 * block + 128].astype(bf16)
    loads[6].wait()
    keys = lax.dot_general(stream, wkv[...], (((1,), (1,)), ((), ())), preferred_element_type=f32)
    for block in range(4):
        zsend_rows[12 + block] = keys[:, 128 * block : 128 * block + 128].astype(bf16)
    quarter = jnp.sum(squares, axis=1, keepdims=True) * 0.25
    high = quarter.astype(bf16)
    low = jnp.where(quarter < jnp.inf, quarter - high.astype(f32), 0.0).astype(bf16)
    zsend_rows[16] = jnp.concatenate(
        [
            keys[:, 512:576].astype(bf16),
            jnp.broadcast_to(high, (TOK, LO_LANE - HI_LANE)),
            jnp.broadcast_to(low, (TOK, 128 - LO_LANE)),
        ],
        axis=1,
    )
    pass_on(pl.ds(8, 9))
    wait_bytes(send.at[:, pl.ds(0, NODES - 1)], send_sem)
    wait_bytes(zrecv, zrecv_sem)

    zrecv_rows = zrecv.reshape(LOCALS, LAT_BLOCKS * OWN, 128)
    total = zrecv_rows[0].astype(f32)
    for source in range(1, LOCALS):
        total = total + zrecv_rows[source].astype(f32)
    last = total[16 * OWN : 17 * OWN]
    square_sum = (last[:, HI_LANE : HI_LANE + 1] + last[:, LO_LANE : LO_LANE + 1]) * 4.0
    finite = square_sum < jnp.inf
    inverse = lax.rsqrt(square_sum / D + EPSILON)
    for block in range(LAT_BLOCKS):
        part = total[OWN * block : OWN * block + OWN]
        part = jnp.where(finite, part * inverse, 0.0).astype(bf16)
        if block < 12:
            q_out[:, 128 * block : 128 * block + 128] = part
        elif block < 16:
            kv_out[:, 128 * block - QL : 128 * block - QL + 128] = part
        else:
            kv_out[:, 512:576] = part[:, 0:64]
    wait_bytes(zrecv.at[pl.ds(0, LOCALS - 1)], zsend_sem)


def write_out(hidden, query, keys, hid_out, q_out, kv_out, sem):
    copies = [
        pltpu.make_async_copy(source, target, sem.at[i])
        for i, (source, target) in enumerate([(hidden, hid_out), (query, q_out), (keys, kv_out)])
    ]
    for copy in copies:
        copy.start()
    for copy in copies:
        copy.wait()


def on_device(expert_ids, slot_gates, expert_rows, residual, norm_gain, w_q_down, w_kv_down):
    anywhere = pl.BlockSpec(memory_space=pl.ANY)
    vmem = pl.BlockSpec(memory_space=pltpu.VMEM)
    shapes = ((TOK, COLS), (OWN, QL), (OWN, KVL))
    results = pl.pallas_call(
        kernel,
        out_shape=tuple(pltpu.VMEM(shape, bf16) for shape in shapes),
        in_specs=[anywhere] * 7,
        out_specs=(vmem,) * 3,
        scratch_shapes=[
            pltpu.VMEM((8, TOK), jnp.int32),
            pltpu.VMEM((2, SLOTS), f32),
            pltpu.VMEM((SLOTS, 2, COLS), bf16),
            pltpu.VMEM((TOK, COLS), bf16),
            pltpu.VMEM((COLS,), f32),
            pltpu.VMEM((COLS, QL), bf16),
            pltpu.VMEM((KVL, COLS), bf16),
            pltpu.VMEM((BLOCKS, NODES, 2, 128), bf16),
            pltpu.VMEM((BLOCKS, NODES, 2, 128), bf16),
            pltpu.VMEM((TOK, COLS), bf16),
            pltpu.VMEM((LAT_BLOCKS, LOCALS, OWN, 128), bf16),
            pltpu.VMEM((LOCALS, LAT_BLOCKS, OWN, 128), bf16),
            pltpu.SemaphoreType.DMA((7,)),
            pltpu.SemaphoreType.DMA,
            pltpu.SemaphoreType.DMA,
            pltpu.SemaphoreType.DMA,
            pltpu.SemaphoreType.DMA,
        ],
        compiler_params=pltpu.CompilerParams(
            collective_id=0, has_side_effects=True, vmem_limit_bytes=56 * 1024 * 1024
        ),
        name="combine_norm_project",
    )(
        expert_ids.T, slot_gates, expert_rows, residual, norm_gain, w_q_down,
        w_kv_down.T,
    )
    return pl.pallas_call(
        write_out,
        out_shape=tuple(jax.ShapeDtypeStruct(shape, bf16) for shape in shapes),
        in_specs=[vmem] * 3,
        out_specs=(anywhere,) * 3,
        scratch_shapes=[pltpu.SemaphoreType.DMA((3,))],
        name="write_out",
    )(*results)


def solution(mesh):
    return jax.shard_map(
        on_device,
        mesh=mesh,
        in_specs=(
            P("node", None),
            P("node", None, None),
            P("node", None, None, "local"),
            P("node", "local"),
            P("local"),
            P("local", None),
            P("local", None),
        ),
        out_specs=(P("node", "local"), P(("node", "local"), None), P(("node", "local"), None)),
        check_vma=False,
    )
```

```python
import jax
import jax.numpy as jnp
from jax import lax
from jax.experimental import pallas as pl
from jax.experimental.pallas import tpu as pltpu
from jax.sharding import PartitionSpec as P

D = 7168
QL = 1536
KVL = 576
TOK = 32
OWN = 4
NODES = 128
SLOTS = 256
COLS = 896
BLOCKS = COLS // 128
LAT_BLOCKS = 17
LOCALS = 8
HI_LANE = 64
LO_LANE = 96
EPSILON = 1e-06
f32, bf16 = jnp.float32, jnp.bfloat16
MESH = pl.DeviceIdType.MESH


def hops(shift):
    return min(shift, 8 - shift)


SHIFTS = sorted(
    ((y, x) for y in range(8) for x in range(8) if (y, x) != (0, 0)),
    key=lambda shift: (-hops(shift[0]) - hops(shift[1]), (shift[0] * 3 + shift[1] * 5) % 8),
)
PER_WORD = 5
WORDS = [
    (
        sum((8 * y + x) << (6 * place) for place, (y, x) in enumerate(SHIFTS[at : at + PER_WORD])),
        len(SHIFTS[at : at + PER_WORD]),
    )
    for at in range(0, len(SHIFTS), PER_WORD)
]


def for_others(me, visit):
    y, x = me >> 4, (me >> 1) & 7
    for word, count in WORDS:

        def step(place, carry, word=word):
            shift = (jnp.int32(word) >> (6 * place)) & 63
            chip = (((y + (shift >> 3)) & 7) << 4) | (((x + shift) & 7) << 1)
            visit(chip | ((me + 1) & 1))
            visit(chip | (me & 1))
            return carry

        lax.fori_loop(0, count, step, 0)
    visit(me ^ 1)


def wait_bytes(ref, sem):
    pltpu.make_async_copy(ref, ref, sem).wait()


def kernel(
    ids_hbm, gates_hbm, rows_hbm, res_hbm, gain_hbm, wq_hbm, wkv_hbm,
    hid_out, q_out, kv_out,
    ids, gates, rows, res, gain, wq, wkv, send, recv, scaled, zsend, zrecv,
    in_sem, above_sem, send_sem, recv_sem, zsend_sem, zrecv_sem,
):
    me = lax.axis_index("node")
    z = lax.axis_index("local")
    loads = [
        pltpu.make_async_copy(source, target, in_sem.at[i])
        for i, (source, target) in enumerate(
            [
                (gates_hbm.at[0], gates), (rows_hbm.at[0], rows), (ids_hbm, ids), (res_hbm, res),
                (gain_hbm, gain), (wq_hbm, wq), (wkv_hbm, wkv),
            ]
        )
    ]
    for load in loads:
        load.start()

    barrier = pltpu.get_barrier_semaphore()

    def greet(other):
        pl.semaphore_signal(barrier, inc=1, device_id={"node": other}, device_id_type=MESH)

    for_others(me, greet)
    for k in range(1, LOCALS):

        @pl.when(z + k < LOCALS)
        def _():
            pl.semaphore_signal(barrier, inc=1, device_id={"local": z + k}, device_id_type=MESH)

    loads[0].wait()
    gate_columns = jnp.concatenate([gates[...], jnp.zeros((6, SLOTS), f32)], axis=0).T
    loads[1].wait()
    pairs = rows[...].astype(f32)
    weighted = pairs[:, 0, :] * gate_columns[:, 0:1] + pairs[:, 1, :] * gate_columns[:, 1:2]
    send_rows = send.reshape(BLOCKS, SLOTS, 128)
    for block in range(BLOCKS):
        send_rows[block] = weighted[:, 128 * block : 128 * block + 128].astype(bf16)

    pl.semaphore_wait(barrier, NODES - 1 + z)
    for k in range(1, LOCALS):

        @pl.when(z >= k)
        def _():
            pl.semaphore_signal(above_sem, inc=1, device_id={"local": z - k}, device_id_type=MESH)

    def push(other):
        pltpu.make_async_remote_copy(
            src_ref=send.at[:, other], dst_ref=recv.at[:, me], send_sem=send_sem, recv_sem=recv_sem,
            device_id={"node": other}, device_id_type=MESH,
        ).start()

    for_others(me, push)
    pltpu.make_async_copy(send.at[:, me], recv.at[:, me], recv_sem).start()

    for load in loads[2:5]:
        load.wait()
    slot = lax.broadcasted_iota(jnp.int32, (SLOTS, TOK), 0)
    nodes = ids[...] >> 1
    routed = nodes[0:1, :] == (slot >> 1)
    for entry in range(1, 8):
        routed = routed | (nodes[entry : entry + 1, :] == (slot >> 1))
    earlier = (
        lax.broadcasted_iota(jnp.int32, (TOK, TOK), 0)
        < lax.broadcasted_iota(jnp.int32, (TOK, TOK), 1)
    ).astype(bf16)
    rank = jnp.dot(routed.astype(bf16), earlier, preferred_element_type=f32)
    serves = (routed & (rank == (slot & 1).astype(f32))).astype(bf16)

    wait_bytes(recv, recv_sem)
    recv_rows = recv.reshape(BLOCKS, SLOTS, 128)
    squares = jnp.zeros((TOK, 128), f32)
    for block in range(BLOCKS):
        cols = slice(128 * block, 128 * block + 128)
        combined = lax.dot_general(
            serves, recv_rows[block], (((0,), (0,)), ((), ())), preferred_element_type=f32
        )
        hidden = (res[:, cols].astype(f32) + combined).astype(bf16)
        hid_out[:, cols] = hidden
        hidden = hidden.astype(f32)
        squares = squares + hidden * hidden
        scaled[:, cols] = (hidden * gain[cols][None, :]).astype(bf16)

    loads[5].wait()
    zsend_rows = zsend.reshape(LAT_BLOCKS, TOK, 128)

    def pass_on(blocks):
        for place in range(LOCALS - 1):
            other = place + (place >= z).astype(jnp.int32)
            pltpu.make_async_remote_copy(
                src_ref=zsend.at[blocks, other], dst_ref=zrecv.at[z, blocks], send_sem=zsend_sem,
                recv_sem=zrecv_sem, device_id={"local": other}, device_id_type=MESH,
            ).start()
        pltpu.make_async_copy(zsend.at[blocks, z], zrecv.at[z, blocks], zrecv_sem).start()


    @pl.when(z < LOCALS - 1)
    def _():
        pl.semaphore_wait(above_sem, LOCALS - 1 - z)

    stream = scaled[...]
    query = jnp.dot(stream, wq[:, 0:1024], preferred_element_type=f32)
    for block in range(8):
        zsend_rows[block] = query[:, 128 * block : 128 * block + 128].astype(bf16)
    pass_on(pl.ds(0, 8))
    query = jnp.dot(stream, wq[:, 1024:QL], preferred_element_type=f32)
    for block in range(4):
        zsend_rows[8 + block] = query[:, 128 * block : 128 * block + 128].astype(bf16)
    loads[6].wait()
    keys = lax.dot_general(stream, wkv[...], (((1,), (1,)), ((), ())), preferred_element_type=f32)
    for block in range(4):
        zsend_rows[12 + block] = keys[:, 128 * block : 128 * block + 128].astype(bf16)
    quarter = jnp.sum(squares, axis=1, keepdims=True) * 0.25
    high = quarter.astype(bf16)
    low = jnp.where(quarter < jnp.inf, quarter - high.astype(f32), 0.0).astype(bf16)
    zsend_rows[16] = jnp.concatenate(
        [
            keys[:, 512:576].astype(bf16),
            jnp.broadcast_to(high, (TOK, LO_LANE - HI_LANE)),
            jnp.broadcast_to(low, (TOK, 128 - LO_LANE)),
        ],
        axis=1,
    )
    pass_on(pl.ds(8, 9))
    wait_bytes(send.at[:, pl.ds(0, NODES - 1)], send_sem)
    wait_bytes(zrecv, zrecv_sem)

    zrecv_rows = zrecv.reshape(LOCALS, LAT_BLOCKS * OWN, 128)
    total = zrecv_rows[0].astype(f32)
    for source in range(1, LOCALS):
        total = total + zrecv_rows[source].astype(f32)
    last = total[16 * OWN : 17 * OWN]
    square_sum = (last[:, HI_LANE : HI_LANE + 1] + last[:, LO_LANE : LO_LANE + 1]) * 4.0
    finite = square_sum < jnp.inf
    inverse = lax.rsqrt(square_sum / D + EPSILON)
    for block in range(LAT_BLOCKS):
        part = total[OWN * block : OWN * block + OWN]
        part = jnp.where(finite, part * inverse, 0.0).astype(bf16)
        if block < 12:
            q_out[:, 128 * block : 128 * block + 128] = part
        elif block < 16:
            kv_out[:, 128 * block - QL : 128 * block - QL + 128] = part
        else:
            kv_out[:, 512:576] = part[:, 0:64]
    wait_bytes(zrecv.at[pl.ds(0, LOCALS - 1)], zsend_sem)


def write_out(hidden, query, keys, hid_out, q_out, kv_out, sem):
    copies = [
        pltpu.make_async_copy(source, target, sem.at[i])
        for i, (source, target) in enumerate([(hidden, hid_out), (query, q_out), (keys, kv_out)])
    ]
    for copy in copies:
        copy.start()
    for copy in copies:
        copy.wait()


def on_device(expert_ids, slot_gates, expert_rows, residual, norm_gain, w_q_down, w_kv_down):
    anywhere = pl.BlockSpec(memory_space=pl.ANY)
    vmem = pl.BlockSpec(memory_space=pltpu.VMEM)
    shapes = ((TOK, COLS), (OWN, QL), (OWN, KVL))
    results = pl.pallas_call(
        kernel,
        out_shape=tuple(pltpu.VMEM(shape, bf16) for shape in shapes),
        in_specs=[anywhere] * 7,
        out_specs=(vmem,) * 3,
        scratch_shapes=[
            pltpu.VMEM((8, TOK), jnp.int32),
            pltpu.VMEM((2, SLOTS), f32),
            pltpu.VMEM((SLOTS, 2, COLS), bf16),
            pltpu.VMEM((TOK, COLS), bf16),
            pltpu.VMEM((COLS,), f32),
            pltpu.VMEM((COLS, QL), bf16),
            pltpu.VMEM((KVL, COLS), bf16),
            pltpu.VMEM((BLOCKS, NODES, 2, 128), bf16),
            pltpu.VMEM((BLOCKS, NODES, 2, 128), bf16),
            pltpu.VMEM((TOK, COLS), bf16),
            pltpu.VMEM((LAT_BLOCKS, LOCALS, OWN, 128), bf16),
            pltpu.VMEM((LOCALS, LAT_BLOCKS, OWN, 128), bf16),
            pltpu.SemaphoreType.DMA((7,)),
            pltpu.SemaphoreType.REGULAR,
            pltpu.SemaphoreType.DMA,
            pltpu.SemaphoreType.DMA,
            pltpu.SemaphoreType.DMA,
            pltpu.SemaphoreType.DMA,
        ],
        compiler_params=pltpu.CompilerParams(
            collective_id=0, has_side_effects=True, vmem_limit_bytes=56 * 1024 * 1024
        ),
        name="combine_norm_project",
    )(
        expert_ids.T, slot_gates, expert_rows, residual, norm_gain, w_q_down,
        w_kv_down.T,
    )
    results = [pltpu.with_memory_space_constraint(result, pltpu.VMEM) for result in results]
    return pl.pallas_call(
        write_out,
        out_shape=tuple(jax.ShapeDtypeStruct(shape, bf16) for shape in shapes),
        in_specs=[vmem] * 3,
        out_specs=(anywhere,) * 3,
        scratch_shapes=[pltpu.SemaphoreType.DMA((3,))],
        compiler_params=pltpu.CompilerParams(vmem_limit_bytes=1024 * 1024),
        name="write_out",
    )(*results)


def solution(mesh):
    return jax.shard_map(
        on_device,
        mesh=mesh,
        in_specs=(
            P("node", None),
            P("node", None, None),
            P("node", None, None, "local"),
            P("node", "local"),
            P("local"),
            P("local", None),
            P("local", None),
        ),
        out_specs=(P("node", "local"), P(("node", "local"), None), P(("node", "local"), None)),
        check_vma=False,
    )
```

```python
import jax
import jax.numpy as jnp
from jax import lax
from jax.experimental import pallas as pl
from jax.experimental.pallas import tpu as pltpu
from jax.sharding import PartitionSpec as P

D = 7168
QL = 1536
KVL = 576
TOK = 32
OWN = 4
NODES = 128
SLOTS = 256
COLS = 896
BLOCKS = COLS // 128
LAT_BLOCKS = 17
LOCALS = 8
HI_LANE = 64
LO_LANE = 96
EPSILON = 1e-06
f32, bf16 = jnp.float32, jnp.bfloat16
MESH = pl.DeviceIdType.MESH


def hops(shift):
    return min(shift, 8 - shift)


FIRST = 32


def turned(shift):
    turns = []
    for _ in range(4):
        if shift not in turns:
            turns.append(shift)
        shift = (shift[1], -shift[0] % 8)
    return turns


SHIFTS = []
for first in sorted(
    ((y, x) for y in range(8) for x in range(8) if (y, x) != (0, 0)),
    key=lambda shift: (-hops(shift[0]) - hops(shift[1]), abs(hops(shift[0]) - hops(shift[1])), shift),
):
    SHIFTS += [shift for shift in turned(first) if shift not in SHIFTS]


def for_others(me, visit, shifts=SHIFTS, own_chip=True):
    y, x, core = me >> 4, (me >> 1) & 7, me & 1
    for shift_y, shift_x in shifts:
        chip = (((y + shift_y) & 7) << 4) | (((x + shift_x) & 7) << 1)
        visit(chip | (1 - core))
        visit(chip | core)
    if own_chip:
        visit(me ^ 1)


def wait_bytes(ref, sem):
    pltpu.make_async_copy(ref, ref, sem).wait()


def kernel(
    ids_hbm, gates_hbm, rows_hbm, res_hbm, gain_hbm, wq_hbm, wkv_hbm,
    hid_out, q_out, kv_out,
    ids, gates, rows, res, gain, wq, wkv, send, recv, scaled, zsend, zrecv,
    in_sem, above_sem, send_sem, recv_sem, zsend_sem, zrecv_sem,
):
    me = lax.axis_index("node")
    z = lax.axis_index("local")
    loads = [
        pltpu.make_async_copy(source, target, in_sem.at[i])
        for i, (source, target) in enumerate(
            [
                (gates_hbm.at[0], gates), (rows_hbm.at[0], rows), (ids_hbm, ids), (res_hbm, res),
                (gain_hbm, gain), (wq_hbm, wq), (wkv_hbm, wkv),
            ]
        )
    ]
    for load in loads[:2]:
        load.start()

    barrier = pltpu.get_barrier_semaphore()

    def greet(other):
        pl.semaphore_signal(barrier, inc=1, device_id={"node": other}, device_id_type=MESH)

    for_others(me, greet)
    for k in range(1, LOCALS):

        @pl.when(z + k < LOCALS)
        def _():
            pl.semaphore_signal(barrier, inc=1, device_id={"local": z + k}, device_id_type=MESH)

    for load in loads[2:]:
        load.start()

    loads[0].wait()
    gate_columns = jnp.concatenate([gates[...], jnp.zeros((6, SLOTS), f32)], axis=0).T
    loads[1].wait()
    pairs = rows[...].astype(f32)
    weighted = pairs[:, 0, :] * gate_columns[:, 0:1] + pairs[:, 1, :] * gate_columns[:, 1:2]
    send_rows = send.reshape(BLOCKS, SLOTS, 128)
    for block in range(BLOCKS):
        send_rows[block] = weighted[:, 128 * block : 128 * block + 128].astype(bf16)

    pl.semaphore_wait(barrier, NODES - 1 + z)

    def push(other):
        pltpu.make_async_remote_copy(
            src_ref=send.at[:, other], dst_ref=recv.at[:, me], send_sem=send_sem, recv_sem=recv_sem,
            device_id={"node": other}, device_id_type=MESH,
        ).start()

    for_others(me, push, SHIFTS[:FIRST], own_chip=False)
    for k in range(1, LOCALS):

        @pl.when(z >= k)
        def _():
            pl.semaphore_signal(above_sem, inc=1, device_id={"local": z - k}, device_id_type=MESH)

    for_others(me, push, SHIFTS[FIRST:])
    pltpu.make_async_copy(send.at[:, me], recv.at[:, me], recv_sem).start()

    for load in loads[2:5]:
        load.wait()
    slot = lax.broadcasted_iota(jnp.int32, (SLOTS, 128), 0)
    nodes = jnp.concatenate([ids[...] >> 1, jnp.zeros((8, 128 - TOK), jnp.int32)], axis=1)
    routed = nodes[0:1, :] == (slot >> 1)
    for entry in range(1, 8):
        routed = routed | (nodes[entry : entry + 1, :] == (slot >> 1))
    earlier = (
        lax.broadcasted_iota(jnp.int32, (128, 128), 0)
        < lax.broadcasted_iota(jnp.int32, (128, 128), 1)
    ).astype(bf16)
    rank = jnp.dot(routed.astype(bf16), earlier, preferred_element_type=f32)
    serves = (routed & (rank == (slot & 1).astype(f32))).astype(f32).T[0:TOK].astype(bf16)

    wait_bytes(recv, recv_sem)
    recv_rows = recv.reshape(BLOCKS, SLOTS, 128)
    squares = jnp.zeros((TOK, 128), f32)
    for block in range(BLOCKS):
        cols = slice(128 * block, 128 * block + 128)
        combined = jnp.dot(serves, recv_rows[block], preferred_element_type=f32)
        hidden = (res[:, cols].astype(f32) + combined).astype(bf16)
        hid_out[:, cols] = hidden
        hidden = hidden.astype(f32)
        squares = squares + hidden * hidden
        scaled[:, cols] = (hidden * gain[cols][None, :]).astype(bf16)

    loads[5].wait()
    zsend_rows = zsend.reshape(LAT_BLOCKS, TOK, 128)

    def pass_on(blocks):
        for place in range(LOCALS - 1):
            other = place + (place >= z).astype(jnp.int32)
            pltpu.make_async_remote_copy(
                src_ref=zsend.at[blocks, other], dst_ref=zrecv.at[z, blocks], send_sem=zsend_sem,
                recv_sem=zrecv_sem, device_id={"local": other}, device_id_type=MESH,
            ).start()
        pltpu.make_async_copy(zsend.at[blocks, z], zrecv.at[z, blocks], zrecv_sem).start()


    @pl.when(z < LOCALS - 1)
    def _():
        pl.semaphore_wait(above_sem, LOCALS - 1 - z)

    stream = scaled[...]
    query = jnp.dot(stream, wq[:, 0:1024], preferred_element_type=f32)
    for block in range(8):
        zsend_rows[block] = query[:, 128 * block : 128 * block + 128].astype(bf16)
    pass_on(pl.ds(0, 8))
    query = jnp.dot(stream, wq[:, 1024:QL], preferred_element_type=f32)
    for block in range(4):
        zsend_rows[8 + block] = query[:, 128 * block : 128 * block + 128].astype(bf16)
    loads[6].wait()
    keys = lax.dot_general(stream, wkv[...], (((1,), (1,)), ((), ())), preferred_element_type=f32)
    for block in range(4):
        zsend_rows[12 + block] = keys[:, 128 * block : 128 * block + 128].astype(bf16)
    quarter = jnp.sum(squares, axis=1, keepdims=True) * 0.25
    high = quarter.astype(bf16)
    low = jnp.where(quarter < jnp.inf, quarter - high.astype(f32), 0.0).astype(bf16)
    zsend_rows[16] = jnp.concatenate(
        [
            keys[:, 512:576].astype(bf16),
            jnp.broadcast_to(high, (TOK, LO_LANE - HI_LANE)),
            jnp.broadcast_to(low, (TOK, 128 - LO_LANE)),
        ],
        axis=1,
    )
    pass_on(pl.ds(8, 9))
    wait_bytes(send.at[:, pl.ds(0, NODES - 1)], send_sem)
    wait_bytes(zrecv, zrecv_sem)

    zrecv_rows = zrecv.reshape(LOCALS, LAT_BLOCKS * OWN, 128)
    total = zrecv_rows[0].astype(f32)
    for source in range(1, LOCALS):
        total = total + zrecv_rows[source].astype(f32)
    last = total[16 * OWN : 17 * OWN]
    square_sum = (last[:, HI_LANE : HI_LANE + 1] + last[:, LO_LANE : LO_LANE + 1]) * 4.0
    finite = square_sum < jnp.inf
    inverse = lax.rsqrt(square_sum / D + EPSILON)
    for block in range(LAT_BLOCKS):
        part = total[OWN * block : OWN * block + OWN]
        part = jnp.where(finite, part * inverse, 0.0).astype(bf16)
        if block < 12:
            q_out[:, 128 * block : 128 * block + 128] = part
        elif block < 16:
            kv_out[:, 128 * block - QL : 128 * block - QL + 128] = part
        else:
            kv_out[:, 512:576] = part[:, 0:64]
    wait_bytes(zrecv.at[pl.ds(0, LOCALS - 1)], zsend_sem)


def write_out(hidden, query, keys, hid_out, q_out, kv_out, sem):
    copies = [
        pltpu.make_async_copy(source, target, sem.at[i])
        for i, (source, target) in enumerate([(hidden, hid_out), (query, q_out), (keys, kv_out)])
    ]
    for copy in copies:
        copy.start()
    for copy in copies:
        copy.wait()


def on_device(expert_ids, slot_gates, expert_rows, residual, norm_gain, w_q_down, w_kv_down):
    anywhere = pl.BlockSpec(memory_space=pl.ANY)
    vmem = pl.BlockSpec(memory_space=pltpu.VMEM)
    shapes = ((TOK, COLS), (OWN, QL), (OWN, KVL))
    results = pl.pallas_call(
        kernel,
        out_shape=tuple(pltpu.VMEM(shape, bf16) for shape in shapes),
        in_specs=[anywhere] * 7,
        out_specs=(vmem,) * 3,
        scratch_shapes=[
            pltpu.VMEM((8, TOK), jnp.int32),
            pltpu.VMEM((2, SLOTS), f32),
            pltpu.VMEM((SLOTS, 2, COLS), bf16),
            pltpu.VMEM((TOK, COLS), bf16),
            pltpu.VMEM((COLS,), f32),
            pltpu.VMEM((COLS, QL), bf16),
            pltpu.VMEM((KVL, COLS), bf16),
            pltpu.VMEM((BLOCKS, NODES, 2, 128), bf16),
            pltpu.VMEM((BLOCKS, NODES, 2, 128), bf16),
            pltpu.VMEM((TOK, COLS), bf16),
            pltpu.VMEM((LAT_BLOCKS, LOCALS, OWN, 128), bf16),
            pltpu.VMEM((LOCALS, LAT_BLOCKS, OWN, 128), bf16),
            pltpu.SemaphoreType.DMA((7,)),
            pltpu.SemaphoreType.REGULAR,
            pltpu.SemaphoreType.DMA,
            pltpu.SemaphoreType.DMA,
            pltpu.SemaphoreType.DMA,
            pltpu.SemaphoreType.DMA,
        ],
        compiler_params=pltpu.CompilerParams(
            collective_id=0, has_side_effects=True, vmem_limit_bytes=56 * 1024 * 1024
        ),
        name="combine_norm_project",
    )(
        expert_ids.T, slot_gates, expert_rows, residual, norm_gain, w_q_down,
        w_kv_down.T,
    )
    results = [pltpu.with_memory_space_constraint(result, pltpu.VMEM) for result in results]
    return pl.pallas_call(
        write_out,
        out_shape=tuple(jax.ShapeDtypeStruct(shape, bf16) for shape in shapes),
        in_specs=[vmem] * 3,
        out_specs=(anywhere,) * 3,
        scratch_shapes=[pltpu.SemaphoreType.DMA((3,))],
        compiler_params=pltpu.CompilerParams(vmem_limit_bytes=1024 * 1024),
        name="write_out",
    )(*results)


def solution(mesh):
    return jax.shard_map(
        on_device,
        mesh=mesh,
        in_specs=(
            P("node", None),
            P("node", None, None),
            P("node", None, None, "local"),
            P("node", "local"),
            P("local"),
            P("local", None),
            P("local", None),
        ),
        out_specs=(P("node", "local"), P(("node", "local"), None), P(("node", "local"), None)),
        check_vma=False,
    )
```

```python
import jax
import jax.numpy as jnp
from jax import lax
from jax.experimental import pallas as pl
from jax.experimental.pallas import tpu as pltpu
from jax.sharding import PartitionSpec as P

D = 7168
QL = 1536
KVL = 576
TOK = 32
OWN = 4
NODES = 128
SLOTS = 256
COLS = 896
BLOCKS = COLS // 128
LAT_BLOCKS = 17
LOCALS = 8
HI_LANE = 64
LO_LANE = 96
EPSILON = 1e-06
f32, bf16 = jnp.float32, jnp.bfloat16
MESH = pl.DeviceIdType.MESH


def hops(shift):
    return min(shift, 8 - shift)


FIRST = 32


def turned(shift):
    turns = []
    for _ in range(4):
        if shift not in turns:
            turns.append(shift)
        shift = (shift[1], -shift[0] % 8)
    return turns


SHIFTS = []
for first in sorted(
    ((y, x) for y in range(8) for x in range(8) if (y, x) != (0, 0)),
    key=lambda shift: (-hops(shift[0]) - hops(shift[1]), abs(hops(shift[0]) - hops(shift[1])), shift),
):
    SHIFTS += [shift for shift in turned(first) if shift not in SHIFTS]


def for_others(me, visit, shifts=SHIFTS, own_chip=True):
    y, x, core = me >> 4, (me >> 1) & 7, me & 1
    for shift_y, shift_x in shifts:
        chip = (((y + shift_y) & 7) << 4) | (((x + shift_x) & 7) << 1)
        visit(chip | (1 - core))
        visit(chip | core)
    if own_chip:
        visit(me ^ 1)


def wait_bytes(ref, sem):
    pltpu.make_async_copy(ref, ref, sem).wait()


def kernel(
    ids_hbm, gates_hbm, rows_hbm, res_hbm, gain_hbm, wq_hbm, wkv_hbm,
    hid_out, q_out, kv_out,
    ids, gates, rows, res, gain, wq, wkv, send, recv, scaled, zsend, zrecv,
    in_sem, above_sem, send_sem, recv_sem, zsend_sem, zrecv_sem,
):
    me = lax.axis_index("node")
    z = lax.axis_index("local")
    loads = [
        pltpu.make_async_copy(source, target, in_sem.at[i])
        for i, (source, target) in enumerate(
            [
                (gates_hbm.at[0], gates), (rows_hbm.at[0], rows), (ids_hbm, ids), (res_hbm, res),
                (gain_hbm, gain), (wq_hbm, wq), (wkv_hbm, wkv),
            ]
        )
    ]
    for load in loads[:2]:
        load.start()

    barrier = pltpu.get_barrier_semaphore()

    def greet(other):
        pl.semaphore_signal(barrier, inc=1, device_id={"node": other}, device_id_type=MESH)

    for_others(me, greet)
    for k in range(1, LOCALS):

        @pl.when(z + k < LOCALS)
        def _():
            pl.semaphore_signal(barrier, inc=1, device_id={"local": z + k}, device_id_type=MESH)

    for load in loads[2:]:
        load.start()

    loads[0].wait()
    gate_columns = jnp.concatenate([gates[...], jnp.zeros((6, SLOTS), f32)], axis=0).T
    loads[1].wait()
    pairs = rows[...].astype(f32)
    weighted = pairs[:, 0, :] * gate_columns[:, 0:1] + pairs[:, 1, :] * gate_columns[:, 1:2]
    send_rows = send.reshape(BLOCKS, SLOTS, 128)
    for block in range(BLOCKS):
        send_rows[block] = weighted[:, 128 * block : 128 * block + 128].astype(bf16)

    pl.semaphore_wait(barrier, NODES - 1 + z)

    def push(other):
        pltpu.make_async_remote_copy(
            src_ref=send.at[:, other], dst_ref=recv.at[:, me], send_sem=send_sem, recv_sem=recv_sem,
            device_id={"node": other}, device_id_type=MESH,
        ).start()

    for_others(me, push, SHIFTS[:FIRST], own_chip=False)
    for k in range(1, LOCALS):

        @pl.when(z >= k)
        def _():
            pl.semaphore_signal(above_sem, inc=1, device_id={"local": z - k}, device_id_type=MESH)

    for_others(me, push, SHIFTS[FIRST:])
    pltpu.make_async_copy(send.at[:, me], recv.at[:, me], recv_sem).start()

    for load in loads[2:5]:
        load.wait()
    slot = lax.broadcasted_iota(jnp.int32, (SLOTS, 128), 0)
    nodes = jnp.concatenate([ids[...] >> 1, jnp.zeros((8, 128 - TOK), jnp.int32)], axis=1)
    routed = nodes[0:1, :] == (slot >> 1)
    for entry in range(1, 8):
        routed = routed | (nodes[entry : entry + 1, :] == (slot >> 1))
    earlier = (
        lax.broadcasted_iota(jnp.int32, (128, 128), 0)
        < lax.broadcasted_iota(jnp.int32, (128, 128), 1)
    ).astype(bf16)
    rank = jnp.dot(routed.astype(bf16), earlier, preferred_element_type=f32)
    serves = (routed & (rank == (slot & 1).astype(f32))).astype(f32).T[0:TOK].astype(bf16)

    wait_bytes(recv, recv_sem)
    recv_rows = recv.reshape(BLOCKS, SLOTS, 128)
    squares = jnp.zeros((TOK, 128), f32)
    for block in range(BLOCKS):
        cols = slice(128 * block, 128 * block + 128)
        combined = jnp.dot(serves, recv_rows[block], preferred_element_type=f32)
        hidden = (res[:, cols].astype(f32) + combined).astype(bf16)
        hid_out[:, cols] = hidden
        hidden = hidden.astype(f32)
        squares = squares + hidden * hidden
        scaled[:, cols] = (hidden * gain[cols][None, :]).astype(bf16)

    loads[5].wait()
    zsend_rows = zsend.reshape(LAT_BLOCKS, TOK, 128)

    def pass_on(blocks):
        for place in range(LOCALS - 1):
            other = place + (place >= z).astype(jnp.int32)
            pltpu.make_async_remote_copy(
                src_ref=zsend.at[blocks, other], dst_ref=zrecv.at[z, blocks], send_sem=zsend_sem,
                recv_sem=zrecv_sem.at[z], device_id={"local": other}, device_id_type=MESH,
            ).start()
        pltpu.make_async_copy(zsend.at[blocks, z], zrecv.at[z, blocks], zrecv_sem.at[z]).start()


    @pl.when(z < LOCALS - 1)
    def _():
        pl.semaphore_wait(above_sem, LOCALS - 1 - z)

    stream = scaled[...]
    query = jnp.dot(stream, wq[:, 0:1024], preferred_element_type=f32)
    for block in range(8):
        zsend_rows[block] = query[:, 128 * block : 128 * block + 128].astype(bf16)
    pass_on(pl.ds(0, 8))
    query = jnp.dot(stream, wq[:, 1024:QL], preferred_element_type=f32)
    for block in range(4):
        zsend_rows[8 + block] = query[:, 128 * block : 128 * block + 128].astype(bf16)
    loads[6].wait()
    keys = lax.dot_general(stream, wkv[...], (((1,), (1,)), ((), ())), preferred_element_type=f32)
    for block in range(4):
        zsend_rows[12 + block] = keys[:, 128 * block : 128 * block + 128].astype(bf16)
    quarter = jnp.sum(squares, axis=1, keepdims=True) * 0.25
    high = quarter.astype(bf16)
    low = jnp.where(quarter < jnp.inf, quarter - high.astype(f32), 0.0).astype(bf16)
    zsend_rows[16] = jnp.concatenate(
        [
            keys[:, 512:576].astype(bf16),
            jnp.broadcast_to(high, (TOK, LO_LANE - HI_LANE)),
            jnp.broadcast_to(low, (TOK, 128 - LO_LANE)),
        ],
        axis=1,
    )
    pass_on(pl.ds(8, 9))
    wait_bytes(send.at[:, pl.ds(0, NODES - 1)], send_sem)

    zrecv_rows = zrecv.reshape(LOCALS, LAT_BLOCKS * OWN, 128)
    total = jnp.zeros((LAT_BLOCKS * OWN, 128), f32)
    for source in range(LOCALS):
        wait_bytes(zrecv.at[source], zrecv_sem.at[source])
        total = total + zrecv_rows[source].astype(f32)
    last = total[16 * OWN : 17 * OWN]
    square_sum = (last[:, HI_LANE : HI_LANE + 1] + last[:, LO_LANE : LO_LANE + 1]) * 4.0
    finite = square_sum < jnp.inf
    inverse = lax.rsqrt(square_sum / D + EPSILON)
    for block in range(LAT_BLOCKS):
        part = total[OWN * block : OWN * block + OWN]
        part = jnp.where(finite, part * inverse, 0.0).astype(bf16)
        if block < 12:
            q_out[:, 128 * block : 128 * block + 128] = part
        elif block < 16:
            kv_out[:, 128 * block - QL : 128 * block - QL + 128] = part
        else:
            kv_out[:, 512:576] = part[:, 0:64]
    wait_bytes(zrecv.at[pl.ds(0, LOCALS - 1)], zsend_sem)


def write_out(hidden, query, keys, hid_out, q_out, kv_out, sem):
    copies = [
        pltpu.make_async_copy(source, target, sem.at[i])
        for i, (source, target) in enumerate([(hidden, hid_out), (query, q_out), (keys, kv_out)])
    ]
    for copy in copies:
        copy.start()
    for copy in copies:
        copy.wait()


def on_device(expert_ids, slot_gates, expert_rows, residual, norm_gain, w_q_down, w_kv_down):
    anywhere = pl.BlockSpec(memory_space=pl.ANY)
    vmem = pl.BlockSpec(memory_space=pltpu.VMEM)
    shapes = ((TOK, COLS), (OWN, QL), (OWN, KVL))
    results = pl.pallas_call(
        kernel,
        out_shape=tuple(pltpu.VMEM(shape, bf16) for shape in shapes),
        in_specs=[anywhere] * 7,
        out_specs=(vmem,) * 3,
        scratch_shapes=[
            pltpu.VMEM((8, TOK), jnp.int32),
            pltpu.VMEM((2, SLOTS), f32),
            pltpu.VMEM((SLOTS, 2, COLS), bf16),
            pltpu.VMEM((TOK, COLS), bf16),
            pltpu.VMEM((COLS,), f32),
            pltpu.VMEM((COLS, QL), bf16),
            pltpu.VMEM((KVL, COLS), bf16),
            pltpu.VMEM((BLOCKS, NODES, 2, 128), bf16),
            pltpu.VMEM((BLOCKS, NODES, 2, 128), bf16),
            pltpu.VMEM((TOK, COLS), bf16),
            pltpu.VMEM((LAT_BLOCKS, LOCALS, OWN, 128), bf16),
            pltpu.VMEM((LOCALS, LAT_BLOCKS, OWN, 128), bf16),
            pltpu.SemaphoreType.DMA((7,)),
            pltpu.SemaphoreType.REGULAR,
            pltpu.SemaphoreType.DMA,
            pltpu.SemaphoreType.DMA,
            pltpu.SemaphoreType.DMA,
            pltpu.SemaphoreType.DMA((LOCALS,)),
        ],
        compiler_params=pltpu.CompilerParams(
            collective_id=0, has_side_effects=True, vmem_limit_bytes=56 * 1024 * 1024
        ),
        name="combine_norm_project",
    )(
        expert_ids.T, slot_gates, expert_rows, residual, norm_gain, w_q_down,
        w_kv_down.T,
    )
    results = [pltpu.with_memory_space_constraint(result, pltpu.VMEM) for result in results]
    return pl.pallas_call(
        write_out,
        out_shape=tuple(jax.ShapeDtypeStruct(shape, bf16) for shape in shapes),
        in_specs=[vmem] * 3,
        out_specs=(anywhere,) * 3,
        scratch_shapes=[pltpu.SemaphoreType.DMA((3,))],
        compiler_params=pltpu.CompilerParams(vmem_limit_bytes=1024 * 1024),
        name="write_out",
    )(*results)


def solution(mesh):
    return jax.shard_map(
        on_device,
        mesh=mesh,
        in_specs=(
            P("node", None),
            P("node", None, None),
            P("node", None, None, "local"),
            P("node", "local"),
            P("local"),
            P("local", None),
            P("local", None),
        ),
        out_specs=(P("node", "local"), P(("node", "local"), None), P(("node", "local"), None)),
        check_vma=False,
    )
```
